768 devices in a mesh: dp: 128 (over z_lo, x, y), mp: 6 (over z_hi, core).
Axes of the slice: x: 4, y: 8, z: 12 (z_hi: 3, z_lo: 4; z = z_hi * 4 + z_lo), core: 2. Of those that a mesh axis runs over, the one named last changes fastest.
Arguments:
- gradient: bfloat16 [6, 768, 24576], P('mp', 'dp'), may hold values from -90 to 90
- left_stat: float32 [6, 24576, 768], P('mp', 'dp'), may hold values from -0.2 to 2.2, as said below
- right_stat: float32 [6, 24576, 768], P('mp', 'dp'), may hold values from -0.2 to 2.2, as said below
- left_root: bfloat16 [6, 24576, 768], P('mp', 'dp'), may hold values from -0.2 to 2.2, as said below
- right_root: bfloat16 [6, 24576, 768], P('mp', 'dp'), may hold values from -0.2 to 2.2, as said below
Outputs:
- update: bfloat16 [6, 768, 24576], P('mp', 'dp')
- left_new: float32 [6, 24576, 768], P('mp', 'dp')
- right_new: float32 [6, 24576, 768], P('mp', 'dp')
The draws below stay inside these ranges and needn't reach their ends.
Inputs may be any that keep to these rules, and one draw needn't show every extreme that they name: `left_stat`: every 768 x 768 block is symmetric. `right_stat`: every 768 x 768 block is symmetric. `left_root`: every 768 x 768 block is symmetric. `right_root`: every 768 x 768 block is symmetric.
All inputs are finite; a program needn't handle non-finite values.
Results may differ from the reference program's by a relative error of at most 0.0049.
Values may be sent and summed in bfloat16 or wider, within the bound.
A program may use at most 32 MiB of HBM per device.

```python
import math
import jax
import jax.numpy as jnp
from jax import lax

BLK = 768
GROUPS = 32
SLABS = 6
WIDTH = 24576


def symmetric_blocks(key, noise, low, high):
    diagonal = jnp.exp(jax.random.uniform(key, (SLABS, GROUPS, BLK, 1), jnp.float32, math.log(low), math.log(high)))
    paired = (noise + jnp.swapaxes(noise, 2, 3)) * (0.25 / math.sqrt(BLK))
    identity = (lax.broadcasted_iota(jnp.int32, (BLK, BLK), 0) == lax.broadcasted_iota(jnp.int32, (BLK, BLK), 1)).astype(jnp.float32)
    return (paired + identity * diagonal).reshape(SLABS, GROUPS * BLK, BLK)


def draw_gradient(key, part):
    key = jax.random.fold_in(key, 11)
    row_key, col_key, noise_key = jax.random.split(key, 3)
    shape = (SLABS, BLK, WIDTH)
    row_scale = jnp.exp(jax.random.uniform(row_key, (SLABS, BLK, 1), jnp.float32) * math.log(10.0))
    col_scale = jnp.exp(jax.random.uniform(col_key, (1, 1, WIDTH), jnp.float32) * math.log(10.0))
    position = jnp.arange(WIDTH, dtype=jnp.float32).reshape(1, 1, WIDTH) / (WIDTH - 1)
    noise = jax.random.truncated_normal(noise_key, -4.0, 4.0, shape, jnp.float32)
    values = 0.067 * row_scale * col_scale * (1.0 + 2.0 * position) * noise
    return values.astype(jnp.bfloat16)


def draw_left_stat(key, part):
    key = jax.random.fold_in(key, 21)
    noise_key, diag_key = jax.random.split(key)
    shape = (SLABS, GROUPS, BLK, BLK)
    noise = jax.random.truncated_normal(noise_key, -4.0, 4.0, shape, jnp.float32)
    return symmetric_blocks(diag_key, noise, 0.5, 2.0)


def draw_right_stat(key, part):
    key = jax.random.fold_in(key, 31)
    noise_key, diag_key = jax.random.split(key)
    shape = (SLABS, GROUPS, BLK, BLK)
    noise = jax.random.truncated_normal(noise_key, -4.0, 4.0, shape, jnp.float32)
    return symmetric_blocks(diag_key, noise, 0.5, 2.0)


def draw_left_root(key, part):
    key = jax.random.fold_in(key, 41)
    noise_key, diag_key = jax.random.split(key)
    shape = (SLABS, GROUPS, BLK, BLK)
    noise = jax.random.truncated_normal(noise_key, -4.0, 4.0, shape, jnp.float32)
    return symmetric_blocks(diag_key, noise, 0.8, 1.6).astype(jnp.bfloat16)


def draw_right_root(key, part):
    key = jax.random.fold_in(key, 51)
    noise_key, diag_key = jax.random.split(key)
    shape = (SLABS, GROUPS, BLK, BLK)
    noise = jax.random.truncated_normal(noise_key, -4.0, 4.0, shape, jnp.float32)
    return symmetric_blocks(diag_key, noise, 0.8, 1.6).astype(jnp.bfloat16)


def setup_inputs(seed: int = 0) -> dict:
    splits = jax.random.split(jax.random.key(seed), 6)
    return {
        "gradient": draw_gradient(jax.random.fold_in(splits[5], 71), 0),
        "left_stat": draw_left_stat(jax.random.fold_in(splits[5], 71), 0),
        "right_stat": draw_right_stat(jax.random.fold_in(splits[5], 71), 0),
        "left_root": draw_left_root(jax.random.fold_in(splits[5], 71), 0),
        "right_root": draw_right_root(jax.random.fold_in(splits[5], 71), 0),
    }


stat_decay = 0.9999
epsilon = 1e-06
clip_rms = 1.0

def block_update(items):
    grad_block, left_block, right_block, lroot_block, rroot_block = items
    left_inc = jnp.dot(grad_block, grad_block.T, preferred_element_type=jnp.float32)
    right_inc = jnp.dot(grad_block.T, grad_block, preferred_element_type=jnp.float32)
    mixed = jnp.dot(grad_block, rroot_block, preferred_element_type=jnp.float32).astype(jnp.bfloat16)
    precond = jnp.dot(lroot_block, mixed, preferred_element_type=jnp.float32)
    grad_square = jnp.mean(jnp.square(grad_block.astype(jnp.float32)))
    prec_square = jnp.mean(jnp.square(precond))
    grafted = precond * jnp.sqrt(grad_square) * lax.rsqrt(prec_square + epsilon)
    left_out = stat_decay * left_block + (1.0 - stat_decay) * left_inc
    right_out = stat_decay * right_block + (1.0 - stat_decay) * right_inc
    return (left_out, right_out, grafted)

def reference(gradient, left_stat, right_stat, left_root, right_root):
    count = SLABS * GROUPS
    grad_blocks = gradient.reshape(SLABS, BLK, GROUPS, BLK).transpose(0, 2, 1, 3).reshape(count, BLK, BLK)
    left_blocks = left_stat.reshape(count, BLK, BLK)
    right_blocks = right_stat.reshape(count, BLK, BLK)
    lroot_blocks = left_root.reshape(count, BLK, BLK)
    rroot_blocks = right_root.reshape(count, BLK, BLK)
    left_out, right_out, grafted = lax.map(block_update, (grad_blocks, left_blocks, right_blocks, lroot_blocks, rroot_blocks))
    total = jnp.mean(jnp.square(grafted))
    factor = jnp.minimum(1.0, clip_rms * lax.rsqrt(total + epsilon))
    scaled = (grafted * factor).astype(jnp.bfloat16)
    update = scaled.reshape(SLABS, GROUPS, BLK, BLK).transpose(0, 2, 1, 3).reshape(SLABS, BLK, GROUPS * BLK)
    left_new = left_out.reshape(SLABS, GROUPS * BLK, BLK)
    right_new = right_out.reshape(SLABS, GROUPS * BLK, BLK)
    return (update, left_new, right_new)
```

```python
import functools

import jax
import jax.numpy as jnp
from jax import lax
from jax.experimental import pallas as pl
from jax.experimental.pallas import tpu as pltpu
from jax.sharding import PartitionSpec as P

MESH = pl.DeviceIdType.MESH
F32 = jnp.float32
BF16 = jnp.bfloat16

BLK = 768
PLANE = 16
RING = 8
SLABS = 6
ROWS = 6
QUART = 192
WIDE = 640
SUBS = 2
CHUNK = PLANE * ROWS
PART = BLK // SUBS

stat_decay = 0.9999
epsilon = 1e-06
clip_rms = 1.0


def iota(shape, dim):
    return lax.broadcasted_iota(jnp.int32, shape, dim)


def by6(v):
    q = (v * 10923) >> 16
    return q, v - q * 6


def one_hot(rows, cols, target):
    return jnp.where(iota((rows, cols), 0) == target(iota((rows, cols), 1)), 1.0, 0.0).astype(BF16)


def dot(a, b):
    return jnp.dot(a, b, preferred_element_type=F32)


def dot_nt(a, b):
    return lax.dot_general(a, b, (((1,), (1,)), ((), ())), preferred_element_type=F32)


def kernel(
    grad, lstat, rstat, lroot, rroot, upd_out, lnew_out, rnew_out,
    upd, lnew, rnew, gin, lold, rold, gsend, recv1, gfull, obuf, tbuf, rrp, lrp, order, cols, leftp, leftq, mixed, gsq, gtrue, ubuf, recvu,
    stat, recvs, msg, recvp, tot, recvt, coef, send2, recv2,
    sload, sstore, s1, r1, sx, rx, sr, rr, sl, rl, st, rt, su, ru, ss, rs, sp, rp, sm, rm, s2, r2,
):
    me = lax.axis_index("dp")
    mp = lax.axis_index("mp")
    p = me // RING
    y = me % RING
    lane = y % 4
    half = y // 4
    parity = y % 2
    upper = lane // 2

    def plane_id(off):
        t = (p + off) % PLANE
        return t, (t * RING + y, mp)

    def ring_id(off):
        t = (y + off) % RING
        return t, (p * RING + t, mp)

    def mp_id(off):
        return (me, (mp + off) % SLABS)

    def remote(src, dst, send, recv, where):
        return pltpu.make_async_remote_copy(
            src_ref=src, dst_ref=dst, send_sem=send, recv_sem=recv, device_id=where, device_id_type=MESH
        )

    loads = [
        pltpu.make_async_copy(src, dst, sload.at[i])
        for i, (src, dst) in enumerate(
            ((grad, gin), (rroot, rrp.at[parity]), (lroot, lrp.at[upper]), (lstat, lold), (rstat, rold))
        )
    ]
    loads[0].start()
    barrier = pltpu.get_barrier_semaphore()
    peers = [plane_id(o)[1] for o in range(1, PLANE)]
    peers += [ring_id(o)[1] for o in range(1, RING)]
    peers += [mp_id(o) for o in range(1, SLABS)]
    for where in peers:
        pl.semaphore_signal(barrier, inc=1, device_id=where, device_id_type=MESH)

    for cp in loads[1:]:
        cp.start()
    gsend[...] = jnp.zeros_like(gsend)
    pl.semaphore_wait(barrier, len(peers))

    def outside(q):
        return (q * QUART + 127) // 128

    def lanes128(k):
        return pl.ds(pl.multiple_of(k * 128, 128), 128)

    def root_copies(kind, src, dst, slot, shift):
        copies = []
        for i in range(1, 6):
            part = lanes128((outside(lane + shift) + i) % 6)
            cp = remote(
                src.at[:, part], dst.at[slot, :, part], sx.at[kind, i], rx.at[kind, i], (me + shift, mp)
            )
            cp.start()
            copies.append(cp)
        return copies

    shift_r, shift_l = 1 - 2 * parity, 2 - 4 * upper
    xr = root_copies(0, rroot, rrp, parity, shift_r)
    xl = root_copies(1, lroot, lrp, upper, shift_l)

    def fill(ref, slot, shift):
        own = outside(lane)
        pick = jnp.where(iota((QUART, BLK), 1) == iota((QUART, BLK), 0) + (lane + shift) * QUART, 1.0, 0.0)
        mine = ref[slot, pl.ds(pl.multiple_of(own * 128 - lane * QUART, 64), 128), :]
        ref[1 - slot, :, lanes128(own)] = dot_nt(pick.astype(BF16), mine).astype(BF16)

    loads[0].wait()
    first = []
    for sub in range(SUBS):
        for q in range(PLANE):
            for h in range(2):
                c = (2 * q + h) * BLK + sub * PART
                gsend[sub, q, 8 * h : 8 * h + ROWS, :] = gin[:, c : c + PART]
        copies = []
        for off in range(1, PLANE):
            t, where = plane_id(off)
            cp = remote(gsend.at[sub, t], recv1.at[sub, p], s1.at[sub, off], r1.at[sub, off], where)
            cp.start()
            copies.append(cp)
        first.append(copies)
        recv1[sub, p] = gsend[sub, p]

    def compact(c):
        i = c & 7
        h = (c >> 3) & 1
        row = jnp.where(h == half, 0, CHUNK) + (c >> 4) * ROWS + i
        return jnp.where(i < ROWS, row, -1)

    def ordered(c):
        q = c >> 5
        yy = (q * 21846) >> 16
        pp, i = by6(c - yy * CHUNK)
        return pp * (RING * ROWS) + yy * ROWS + i

    def by_ring(c):
        s = (c >= QUART).astype(jnp.int32)
        q = ((c >> 4) * 21846) >> 16
        xx = q - 4 * s
        yy, i = by6(c - q * 48)
        return yy * 48 + s * 24 + xx * ROWS + i

    def spread(c):
        h = (c >= 48).astype(jnp.int32)
        q, i = by6(c - 48 * h)
        return q * 16 + h * ROWS + i

    def spread_last(block):
        def row(c):
            h = (c >= 48).astype(jnp.int32)
            q, i = by6(c - 48 * h)
            low = (i >= 3).astype(jnp.int32)
            return jnp.where(i - 3 * low == block, q * 16 + 12 + 2 * h + low, -1)

        return row

    order[...] = one_hot(BLK, BLK, ordered)
    compactor = one_hot(2 * CHUNK, PLANE * 16, compact)
    def hop(way, dist, sub, src):
        step = 1 if way == 0 else RING - 1
        slot = (y + (RING - step) * dist) % RING
        send, recv = (sr, rr) if way == 0 else (sl, rl)
        where = ring_id(step)[1]
        dst = gfull.at[sub, slot]
        return remote(dst if src is None else src, dst, send.at[dist, sub], recv.at[dist + 1, sub], where)

    def transit(way, sub):
        step = 1 if way == 0 else RING - 1
        return remote(
            obuf.at[sub], tbuf.at[way, sub], st.at[way, sub], rt.at[way, sub], ring_id(step)[1]
        )

    def slot_of(way, dist):
        return (y + (RING - 1 if way == 0 else 1) * dist) % RING

    def arrival(way, dist, sub):
        recv = rr if way == 0 else rl
        slot = slot_of(way, dist)
        where = ring_id(1 if way == 0 else RING - 1)[1]
        there = gfull.at[sub, slot]
        remote(there, there, recv.at[dist, sub], recv.at[dist, sub], where).wait_recv()

    def multiply(slot):
        total, squares = 0.0, 0.0
        for sub in range(SUBS):
            chunk = gfull[sub, slot]
            total = total + dot(chunk, cols[PART * sub : PART * sub + PART])
            squares = squares + jnp.sum(jnp.square(chunk.astype(F32)), keepdims=True)
        mixed[slot] = total.astype(BF16)
        gsq[slot] = jnp.broadcast_to(squares, (8, 128))

    ranks = (lane, 3 - lane)
    for sub in range(SUBS):
        for cp in first[sub]:
            cp.wait_recv()
        packed = dot(compactor, recv1[sub].reshape(PLANE * 16, PART)).astype(BF16)
        gfull[sub, y] = packed[:CHUNK]
        obuf[sub] = packed[CHUNK:]
        for way in range(2):

            @pl.when(ranks[way] == 2)
            def _():
                transit(way, sub).start()

        for way in range(2):

            @pl.when(ranks[way] <= 2)
            def _():
                hop(way, 0, sub, None).start()

            @pl.when(ranks[way] == 3)
            def _():
                hop(way, 0, sub, obuf.at[sub]).start()

    for dist in range(1, 6):
        for sub in range(SUBS):
            for way in range(2):
                rank = ranks[way]
                if dist == 1:

                    @pl.when(rank == 3)
                    def _():
                        transit(way, sub).wait_recv()
                        hop(way, 1, sub, tbuf.at[way, sub]).start()

                @pl.when(dist <= rank + 2)
                def _():
                    arrival(way, dist, sub)
                    if dist <= 4:

                        @pl.when(rank <= 2)
                        def _():
                            hop(way, dist, sub, None).start()

        if dist == 3:
            loads[1].wait()
            loads[2].wait()
            for cp in xr:
                cp.wait_recv()
            fill(rrp, parity, shift_r)
            cols[...] = jnp.transpose(rrp[...].reshape(384, BLK))
            for cp in xl:
                cp.wait_recv()
            fill(lrp, upper, shift_l)
            left_rows = dot(one_hot(384, 384, by_ring), lrp[...].reshape(384, BLK)).astype(BF16)
            leftp[...] = left_rows
        if dist < 4:
            continue
        if dist == 4:
            leftq[...] = dot(leftp[...], order[...]).astype(BF16)
            multiply(y)
        for back in (1, 2, 3, 4) if dist == 4 else (dist,):
            for way in range(2):

                @pl.when(back <= ranks[way] + 2)
                def _():
                    multiply(slot_of(way, back))

    direction = dot(leftq[...], mixed[...].reshape(BLK, 384))
    partial = jnp.sum(jnp.square(direction), keepdims=True)
    stat[...] = jnp.where(iota((8, 128), 0) == 0, partial, jnp.sum(gsq[...], axis=0) * 0.25)
    ring_s = []
    for off in range(1, RING):
        t, where = ring_id(off)
        cs = remote(stat, recvs.at[y], ss.at[off], rs.at[off], where)
        cs.start()
        ring_s.append(cs)
    ubuf[...] = direction.astype(BF16).reshape(RING, 48, 384)
    ring_u = []
    for off in (4, 3, 5, 2, 6, 1, 7):
        t, where = ring_id(off)
        cu = remote(ubuf.at[t], recvu.at[y], su.at[off], ru.at[off], where)
        cu.start()
        ring_u.append(cu)
    recvs[y] = stat[...]
    recvu[y] = ubuf[y]

    def reorder(k):
        for sub in range(SUBS):
            gtrue[QUART * k : QUART * k + QUART, PART * sub : PART * sub + PART] = dot(
                order[QUART * k : QUART * k + QUART], gfull[sub].reshape(BLK, PART)
            ).astype(BF16)

    reorder(0)
    reorder(1)

    for cs in ring_s:
        cs.wait_recv()
    for h in range(2):
        msg[h] = recvs[4 * h] + recvs[4 * h + 1] + recvs[4 * h + 2] + recvs[4 * h + 3]
    plane_s = []
    for off in range(1, PLANE):
        t, where = plane_id(off)
        cp = remote(msg, recvp.at[p], sp.at[off], rp.at[off], where)
        cp.start()
        plane_s.append(cp)
    recvp[p] = msg[...]
    reorder(2)
    reorder(3)

    loads[3].wait()
    loads[4].wait()
    rows = gtrue[pl.ds(pl.multiple_of(lane * QUART, QUART), QUART), :]
    lnew[...] = stat_decay * lold[...] + (1.0 - stat_decay) * dot_nt(rows, gtrue[...])
    stores = [pltpu.make_async_copy(lnew, lnew_out, sstore.at[0])]
    stores[0].start()
    pick = jnp.where(iota((QUART, BLK), 1) == iota((QUART, BLK), 0) + lane * QUART, 1.0, 0.0).astype(BF16)
    columns = dot_nt(pick, gtrue[...]).astype(BF16)
    rnew[...] = stat_decay * rold[...] + (1.0 - stat_decay) * dot(columns, gtrue[...])
    stores.append(pltpu.make_async_copy(rnew, rnew_out, sstore.at[1]))
    stores[1].start()

    for cp in first[0] + first[1] + xr + xl:
        cp.wait_send()
    for way in range(2):
        rank = ranks[way]

        @pl.when(rank == 2)
        def _():
            for sub in range(SUBS):
                transit(way, sub).wait_send()

        for dist in range(5):
            count = jnp.where(rank == 3, 2, rank + 3)

            @pl.when(dist < count)
            def _():
                for sub in range(SUBS):
                    hop(way, dist, sub, None).wait_send()

    place = one_hot(128, 96, spread)
    place_last = [one_hot(128, 96, spread_last(block)) for block in range(3)]
    for cu in ring_u:
        cu.wait_recv()
    for e in range(2):
        both = [jnp.concatenate([recvu[2 * k + e], recvu[4 + 2 * k + e]], axis=0) for k in range(2)]
        both = jnp.concatenate(both, axis=1)
        last = jnp.concatenate([dot(at, both[:, WIDE:]) for at in place_last], axis=1)
        out = dot(place, both[:, :WIDE])
        out = jnp.concatenate([out[:, :384] + last, out[:, 384:]], axis=1).astype(BF16)
        for s in range(2):
            for xx in range(4):
                send2[(e + 2 * s) * 4 + xx] = out[(4 * s + xx) * 16 : (4 * s + xx) * 16 + 16]
    second = []
    for off in range(1, PLANE):
        t, where = plane_id(off)
        cp = remote(send2.at[t], recv2.at[p], s2.at[off], r2.at[off], where)
        cp.start()
        second.append(cp)

    for cp in plane_s:
        cp.wait_recv()
    size = float(BLK * BLK)
    square = recvp[:, :, 0:1, :] * (1.0 / size)
    gmean = recvp[:, :, 1:2, :] * (1.0 / size)
    root = lax.rsqrt(square + epsilon)
    slab = jnp.sum(gmean * square * root * root, axis=(0, 1))
    tot[...] = jnp.broadcast_to(slab, (8, 128))
    mp_s = []
    for off in range(1, SLABS):
        cp = remote(tot, recvt.at[mp], sm.at[off], rm.at[off], mp_id(off))
        cp.start()
        mp_s.append(cp)
    recvt[mp] = tot[...]
    recv2[p] = send2[p]

    for cp in ring_s + ring_u + plane_s:
        cp.wait_send()
    for cp in mp_s:
        cp.wait_recv()
    total = jnp.sum(recvt[...], axis=0)[0:1] * (1.0 / float(2 * PLANE * SLABS))
    factor = jnp.minimum(1.0, clip_rms * lax.rsqrt(total + epsilon))
    coef[...] = jnp.sqrt(gmean) * root * factor[None, None]

    def finish(q):
        got = recv2[q].astype(F32)
        for h in range(2):
            c = pl.multiple_of((2 * q + h) * BLK, 128)
            scale = coef[q, h][:, 0:1]
            upd[:, pl.ds(c, WIDE)] = (got[ROWS * h : ROWS * h + ROWS] * scale).astype(BF16)
            last = [got[12 + 2 * h + r : 13 + 2 * h + r, 128 * k : 128 * k + 128] for r in range(2) for k in range(3)]
            upd[:, pl.ds(c + WIDE, 128)] = (jnp.concatenate(last, axis=0) * scale).astype(BF16)

    finish(p)
    for off in range(1, PLANE):
        second[off - 1].wait_recv()
        finish((p + PLANE - off) % PLANE)
    stores.append(pltpu.make_async_copy(upd, upd_out, sstore.at[2]))
    stores[2].start()

    for cp in second + mp_s:
        cp.wait_send()
    for cp in stores:
        cp.wait()


def place_out(upd, lnew, rnew, upd_out, lnew_out, rnew_out, upd_mid, lnew_mid, rnew_mid, sem):
    legs = ((lnew, lnew_mid, lnew_out), (rnew, rnew_mid, rnew_out), (upd, upd_mid, upd_out))
    inward = [pltpu.make_async_copy(a, b, sem.at[0, i]) for i, (a, b, _) in enumerate(legs)]
    outward = [pltpu.make_async_copy(b, c, sem.at[1, i]) for i, (_, b, c) in enumerate(legs)]
    for cp in inward:
        cp.start()
    for there, on in zip(inward, outward):
        there.wait()
        on.start()
    for cp in outward:
        cp.wait()


def on_device(gradient, left_stat, right_stat, left_root, right_root):
    hbm = pl.BlockSpec(memory_space=pltpu.HBM)
    dma = pltpu.SemaphoreType.DMA
    shapes = (
        jax.ShapeDtypeStruct((ROWS, 2 * PLANE * BLK), BF16),
        jax.ShapeDtypeStruct((QUART, BLK), F32),
        jax.ShapeDtypeStruct((QUART, BLK), F32),
    )
    update, left_new, right_new = pl.pallas_call(
        kernel,
        out_shape=shapes,
        in_specs=[hbm] * 5,
        out_specs=(hbm, hbm, hbm),
        scratch_shapes=[
            pltpu.VMEM((ROWS, 2 * PLANE * BLK), BF16),
            pltpu.VMEM((QUART, BLK), F32),
            pltpu.VMEM((QUART, BLK), F32),
            pltpu.VMEM((ROWS, 2 * PLANE * BLK), BF16),
            pltpu.VMEM((QUART, BLK), F32),
            pltpu.VMEM((QUART, BLK), F32),
            pltpu.VMEM((SUBS, PLANE, 16, PART), BF16),
            pltpu.VMEM((SUBS, PLANE, 16, PART), BF16),
            pltpu.VMEM((SUBS, RING, CHUNK, PART), BF16),
            pltpu.VMEM((SUBS, CHUNK, PART), BF16),
            pltpu.VMEM((2, SUBS, CHUNK, PART), BF16),
            pltpu.VMEM((2, QUART, BLK), BF16),
            pltpu.VMEM((2, QUART, BLK), BF16),
            pltpu.VMEM((BLK, BLK), BF16),
            pltpu.VMEM((BLK, 384), BF16),
            pltpu.VMEM((384, BLK), BF16),
            pltpu.VMEM((384, BLK), BF16),
            pltpu.VMEM((RING, CHUNK, 384), BF16),
            pltpu.VMEM((RING, 8, 128), F32),
            pltpu.VMEM((BLK, BLK), BF16),
            pltpu.VMEM((RING, 48, 384), BF16),
            pltpu.VMEM((RING, 48, 384), BF16),
            pltpu.VMEM((8, 128), F32),
            pltpu.VMEM((RING, 8, 128), F32),
            pltpu.VMEM((2, 8, 128), F32),
            pltpu.VMEM((PLANE, 2, 8, 128), F32),
            pltpu.VMEM((8, 128), F32),
            pltpu.VMEM((SLABS, 8, 128), F32),
            pltpu.VMEM((PLANE, 2, 1, 128), F32),
            pltpu.VMEM((PLANE, 16, WIDE), BF16),
            pltpu.VMEM((PLANE, 16, WIDE), BF16),
            dma((5,)),
            dma((3,)),
            dma((SUBS, PLANE)), dma((SUBS, PLANE)),
            dma((2, 6)), dma((2, 6)),
            dma((5, SUBS)), dma((6, SUBS)),
            dma((5, SUBS)), dma((6, SUBS)),
            dma((2, SUBS)), dma((2, SUBS)),
            dma((RING,)), dma((RING,)),
            dma((RING,)), dma((RING,)),
            dma((PLANE,)), dma((PLANE,)),
            dma((SLABS,)), dma((SLABS,)),
            dma((PLANE,)), dma((PLANE,)),
        ],
        compiler_params=pltpu.CompilerParams(
            collective_id=0, has_side_effects=True, vmem_limit_bytes=63 * 1024 * 1024
        ),
    )(gradient[0], left_stat[0], right_stat[0], left_root[0], right_root[0])
    update, left_new, right_new = pl.pallas_call(
        place_out,
        out_shape=shapes,
        in_specs=[hbm] * 3,
        out_specs=(hbm, hbm, hbm),
        scratch_shapes=[
            pltpu.VMEM((ROWS, 2 * PLANE * BLK), BF16),
            pltpu.VMEM((QUART, BLK), F32),
            pltpu.VMEM((QUART, BLK), F32),
            dma((2, 3)),
        ],
        compiler_params=pltpu.CompilerParams(vmem_limit_bytes=63 * 1024 * 1024),
    )(update, left_new, right_new)
    return (update[None], left_new[None], right_new[None])


def solution(mesh):
    spec = P("mp", "dp", None)
    return jax.shard_map(
        on_device, mesh=mesh, in_specs=(spec,) * 5, out_specs=(spec,) * 3, check_vma=False
    )
```

```python
import functools

import jax
import jax.numpy as jnp
from jax import lax
from jax.experimental import pallas as pl
from jax.experimental.pallas import tpu as pltpu
from jax.sharding import PartitionSpec as P

MESH = pl.DeviceIdType.MESH
F32 = jnp.float32
BF16 = jnp.bfloat16

BLK = 768
PLANE = 16
RING = 8
SLABS = 6
ROWS = 6
QUART = 192
WIDE = 640
SUBS = 2
CHUNK = PLANE * ROWS
PART = BLK // SUBS

stat_decay = 0.9999
epsilon = 1e-06
clip_rms = 1.0


def iota(shape, dim):
    return lax.broadcasted_iota(jnp.int32, shape, dim)


def by6(v):
    q = (v * 10923) >> 16
    return q, v - q * 6


def one_hot(rows, cols, target):
    return jnp.where(iota((rows, cols), 0) == target(iota((rows, cols), 1)), 1.0, 0.0).astype(BF16)


def dot(a, b):
    return jnp.dot(a, b, preferred_element_type=F32)


def dot_nt(a, b):
    return lax.dot_general(a, b, (((1,), (1,)), ((), ())), preferred_element_type=F32)


def kernel(
    grad, lstat, rstat, lroot, rroot, upd_out, lnew_out, rnew_out,
    upd, lnew, rnew, gin, lold, rold, gsend, recv1, gfull, obuf, tbuf, rrp, lrp, order, cols, leftp, leftq, mixed, gsq, gtrue, ubuf, recvu,
    stat, recvs, msg, recvp, tot, recvt, coef, send2, recv2,
    sload, sstore, s1, r1, sx, rx, sr, rr, sl, rl, st, rt, su, ru, ss, rs, sp, rp, sm, rm, s2, r2,
):
    me = lax.axis_index("dp")
    mp = lax.axis_index("mp")
    p = me // RING
    y = me % RING
    lane = y % 4
    half = y // 4
    parity = y % 2
    upper = lane // 2

    def plane_id(off):
        t = (p + off) % PLANE
        return t, (t * RING + y, mp)

    def ring_id(off):
        t = (y + off) % RING
        return t, (p * RING + t, mp)

    def mp_id(off):
        return (me, (mp + off) % SLABS)

    def remote(src, dst, send, recv, where):
        return pltpu.make_async_remote_copy(
            src_ref=src, dst_ref=dst, send_sem=send, recv_sem=recv, device_id=where, device_id_type=MESH
        )

    loads = [
        pltpu.make_async_copy(src, dst, sload.at[i])
        for i, (src, dst) in enumerate(
            ((grad, gin), (rroot, rrp.at[parity]), (lroot, lrp.at[upper]), (lstat, lold), (rstat, rold))
        )
    ]
    loads[0].start()
    barrier = pltpu.get_barrier_semaphore()
    peers = [plane_id(o)[1] for o in range(1, PLANE)]
    peers += [ring_id(o)[1] for o in range(1, RING)]
    peers += [mp_id(o) for o in range(1, SLABS)]
    for where in peers:
        pl.semaphore_signal(barrier, inc=1, device_id=where, device_id_type=MESH)

    for cp in loads[1:]:
        cp.start()
    gsend[...] = jnp.zeros_like(gsend)
    pl.semaphore_wait(barrier, len(peers))

    def outside(q):
        return (q * QUART + 127) // 128

    def lanes128(k):
        return pl.ds(pl.multiple_of(k * 128, 128), 128)

    def root_copies(kind, src, dst, slot, shift):
        copies = []
        for i in range(1, 6):
            part = lanes128((outside(lane + shift) + i) % 6)
            cp = remote(
                src.at[:, part], dst.at[slot, :, part], sx.at[kind, i], rx.at[kind, i], (me + shift, mp)
            )
            cp.start()
            copies.append(cp)
        return copies

    shift_r, shift_l = 1 - 2 * parity, 2 - 4 * upper
    xr = root_copies(0, rroot, rrp, parity, shift_r)
    xl = root_copies(1, lroot, lrp, upper, shift_l)

    def fill(ref, slot, shift):
        own = outside(lane)
        pick = jnp.where(iota((QUART, BLK), 1) == iota((QUART, BLK), 0) + (lane + shift) * QUART, 1.0, 0.0)
        mine = ref[slot, pl.ds(pl.multiple_of(own * 128 - lane * QUART, 64), 128), :]
        ref[1 - slot, :, lanes128(own)] = dot_nt(pick.astype(BF16), mine).astype(BF16)

    loads[0].wait()
    first = []
    for sub in range(SUBS):
        for q in range(PLANE):
            for h in range(2):
                c = (2 * q + h) * BLK + sub * PART
                gsend[sub, q, 8 * h : 8 * h + ROWS, :] = gin[:, c : c + PART]
        copies = []
        for off in range(1, PLANE):
            t, where = plane_id(off)
            cp = remote(gsend.at[sub, t], recv1.at[sub, p], s1.at[sub, off], r1.at[sub, off], where)
            cp.start()
            copies.append(cp)
        first.append(copies)
        recv1[sub, p] = gsend[sub, p]

    def compact(c):
        i = c & 7
        h = (c >> 3) & 1
        row = jnp.where(h == half, 0, CHUNK) + (c >> 4) * ROWS + i
        return jnp.where(i < ROWS, row, -1)

    def ordered(c):
        q = c >> 5
        yy = (q * 21846) >> 16
        pp, i = by6(c - yy * CHUNK)
        return pp * (RING * ROWS) + yy * ROWS + i

    def by_ring(c):
        s = (c >= QUART).astype(jnp.int32)
        q = ((c >> 4) * 21846) >> 16
        xx = q - 4 * s
        yy, i = by6(c - q * 48)
        return yy * 48 + s * 24 + xx * ROWS + i

    def spread(c):
        h = (c >= 48).astype(jnp.int32)
        q, i = by6(c - 48 * h)
        return q * 16 + h * ROWS + i

    def spread_last(block):
        def row(c):
            h = (c >= 48).astype(jnp.int32)
            q, i = by6(c - 48 * h)
            low = (i >= 3).astype(jnp.int32)
            return jnp.where(i - 3 * low == block, q * 16 + 12 + 2 * h + low, -1)

        return row

    order[...] = one_hot(BLK, BLK, ordered)
    compactor = one_hot(2 * CHUNK, PLANE * 16, compact)
    def hop(way, dist, sub, src):
        step = 1 if way == 0 else RING - 1
        slot = (y + (RING - step) * dist) % RING
        send, recv = (sr, rr) if way == 0 else (sl, rl)
        where = ring_id(step)[1]
        dst = gfull.at[sub, slot]
        return remote(dst if src is None else src, dst, send.at[dist, sub], recv.at[dist + 1, sub], where)

    def transit(way, sub):
        step = 1 if way == 0 else RING - 1
        return remote(
            obuf.at[sub], tbuf.at[way, sub], st.at[way, sub], rt.at[way, sub], ring_id(step)[1]
        )

    def slot_of(way, dist):
        return (y + (RING - 1 if way == 0 else 1) * dist) % RING

    def arrival(way, dist, sub):
        recv = rr if way == 0 else rl
        slot = slot_of(way, dist)
        where = ring_id(1 if way == 0 else RING - 1)[1]
        there = gfull.at[sub, slot]
        remote(there, there, recv.at[dist, sub], recv.at[dist, sub], where).wait_recv()

    def multiply(slot):
        total, squares = 0.0, 0.0
        for sub in range(SUBS):
            chunk = gfull[sub, slot]
            total = total + dot(chunk, cols[PART * sub : PART * sub + PART])
            squares = squares + jnp.sum(jnp.square(chunk.astype(F32)), keepdims=True)
        mixed[slot] = total.astype(BF16)
        gsq[slot] = jnp.broadcast_to(squares, (8, 128))

    ranks = (lane, 3 - lane)
    for sub in range(SUBS):
        for cp in first[sub]:
            cp.wait_recv()
        packed = dot(compactor, recv1[sub].reshape(PLANE * 16, PART)).astype(BF16)
        gfull[sub, y] = packed[:CHUNK]
        obuf[sub] = packed[CHUNK:]
        for way in range(2):

            @pl.when(ranks[way] == 2)
            def _():
                transit(way, sub).start()

        for way in range(2):

            @pl.when(ranks[way] <= 2)
            def _():
                hop(way, 0, sub, None).start()

            @pl.when(ranks[way] == 3)
            def _():
                hop(way, 0, sub, obuf.at[sub]).start()

    for dist in range(1, 6):
        for sub in range(SUBS):
            for way in range(2):
                rank = ranks[way]
                if dist == 1:

                    @pl.when(rank == 3)
                    def _():
                        transit(way, sub).wait_recv()
                        hop(way, 1, sub, tbuf.at[way, sub]).start()

                @pl.when(dist <= rank + 2)
                def _():
                    arrival(way, dist, sub)
                    if dist <= 4:

                        @pl.when(rank <= 2)
                        def _():
                            hop(way, dist, sub, None).start()

        if dist == 3:
            loads[1].wait()
            loads[2].wait()
            for cp in xr:
                cp.wait_recv()
            fill(rrp, parity, shift_r)
            cols[...] = jnp.transpose(rrp[...].reshape(384, BLK))
            for cp in xl:
                cp.wait_recv()
            fill(lrp, upper, shift_l)
            left_rows = dot(one_hot(384, 384, by_ring), lrp[...].reshape(384, BLK)).astype(BF16)
            leftp[...] = left_rows
        if dist < 4:
            continue
        if dist == 4:
            leftq[...] = dot(leftp[...], order[...]).astype(BF16)
            multiply(y)
        for back in (1, 2, 3, 4) if dist == 4 else (dist,):
            for way in range(2):

                @pl.when(back <= ranks[way] + 2)
                def _():
                    multiply(slot_of(way, back))

    direction = dot(leftq[...], mixed[...].reshape(BLK, 384))
    partial = jnp.sum(jnp.square(direction), keepdims=True)
    stat[...] = jnp.where(iota((8, 128), 0) == 0, partial, jnp.sum(gsq[...], axis=0) * 0.25)
    ring_s = []
    for off in range(1, RING):
        t, where = ring_id(off)
        cs = remote(stat, recvs.at[y], ss.at[off], rs.at[off], where)
        cs.start()
        ring_s.append(cs)
    ubuf[...] = direction.astype(BF16).reshape(RING, 48, 384)
    ring_u = []
    for off in (4, 2, 6, 3, 5, 1, 7):
        t, where = ring_id(off)
        cu = remote(ubuf.at[t], recvu.at[y], su.at[off], ru.at[off], where)
        cu.start()
        ring_u.append(cu)
    recvs[y] = stat[...]
    recvu[y] = ubuf[y]

    def reorder(k):
        for sub in range(SUBS):
            gtrue[QUART * k : QUART * k + QUART, PART * sub : PART * sub + PART] = dot(
                order[QUART * k : QUART * k + QUART], gfull[sub].reshape(BLK, PART)
            ).astype(BF16)

    reorder(0)
    reorder(1)

    for cs in ring_s:
        cs.wait_recv()
    for h in range(2):
        msg[h] = recvs[4 * h] + recvs[4 * h + 1] + recvs[4 * h + 2] + recvs[4 * h + 3]
    plane_s = []
    for off in range(1, PLANE):
        t, where = plane_id(off)
        cp = remote(msg, recvp.at[p], sp.at[off], rp.at[off], where)
        cp.start()
        plane_s.append(cp)
    recvp[p] = msg[...]
    reorder(2)
    reorder(3)

    loads[3].wait()
    loads[4].wait()
    rows = gtrue[pl.ds(pl.multiple_of(lane * QUART, QUART), QUART), :]
    lnew[...] = stat_decay * lold[...] + (1.0 - stat_decay) * dot_nt(rows, gtrue[...])
    stores = [pltpu.make_async_copy(lnew, lnew_out, sstore.at[0])]
    stores[0].start()
    pick = jnp.where(iota((QUART, BLK), 1) == iota((QUART, BLK), 0) + lane * QUART, 1.0, 0.0).astype(BF16)
    columns = dot_nt(pick, gtrue[...]).astype(BF16)
    rnew[...] = stat_decay * rold[...] + (1.0 - stat_decay) * dot(columns, gtrue[...])
    stores.append(pltpu.make_async_copy(rnew, rnew_out, sstore.at[1]))
    stores[1].start()

    for cp in first[0] + first[1] + xr + xl:
        cp.wait_send()
    for way in range(2):
        rank = ranks[way]

        @pl.when(rank == 2)
        def _():
            for sub in range(SUBS):
                transit(way, sub).wait_send()

        for dist in range(5):
            count = jnp.where(rank == 3, 2, rank + 3)

            @pl.when(dist < count)
            def _():
                for sub in range(SUBS):
                    hop(way, dist, sub, None).wait_send()

    place = one_hot(128, 96, spread)
    place_last = [one_hot(128, 96, spread_last(block)) for block in range(3)]
    second = []
    for off in range(1, PLANE):
        t, where = plane_id(off)
        second.append(remote(send2.at[t], recv2.at[p], s2.at[off], r2.at[off], where))

    for group in range(2):
        e = (parity + group) % 2
        for cu in ring_u[:3] if group == 0 else ring_u[3:]:
            cu.wait_recv()
        both = [jnp.concatenate([recvu[2 * k + e], recvu[4 + 2 * k + e]], axis=0) for k in range(2)]
        both = jnp.concatenate(both, axis=1)
        last = jnp.concatenate([dot(at, both[:, WIDE:]) for at in place_last], axis=1)
        out = dot(place, both[:, :WIDE])
        out = jnp.concatenate([out[:, :384] + last, out[:, 384:]], axis=1).astype(BF16)
        for s in range(2):
            for xx in range(4):
                send2[(e + 2 * s) * 4 + xx] = out[(4 * s + xx) * 16 : (4 * s + xx) * 16 + 16]
        z, x = p // 4, p % 4
        for s in (1, 0):
            for dx in (2, 1, 3, 0):
                t = (z + (e + z) % 2 + 2 * s) % 4 * 4 + (x + dx) % 4
                off = (t + PLANE - p) % PLANE

                @pl.when(off > 0)
                def _():
                    remote(send2.at[t], recv2.at[p], s2.at[off], r2.at[off], (t * RING + y, mp)).start()

    for cp in plane_s:
        cp.wait_recv()
    size = float(BLK * BLK)
    square = recvp[:, :, 0:1, :] * (1.0 / size)
    gmean = recvp[:, :, 1:2, :] * (1.0 / size)
    root = lax.rsqrt(square + epsilon)
    slab = jnp.sum(gmean * square * root * root, axis=(0, 1))
    tot[...] = jnp.broadcast_to(slab, (8, 128))
    mp_s = []
    for off in range(1, SLABS):
        cp = remote(tot, recvt.at[mp], sm.at[off], rm.at[off], mp_id(off))
        cp.start()
        mp_s.append(cp)
    recvt[mp] = tot[...]
    recv2[p] = send2[p]

    for cp in ring_s + ring_u + plane_s:
        cp.wait_send()
    for cp in mp_s:
        cp.wait_recv()
    total = jnp.sum(recvt[...], axis=0)[0:1] * (1.0 / float(2 * PLANE * SLABS))
    factor = jnp.minimum(1.0, clip_rms * lax.rsqrt(total + epsilon))
    coef[...] = jnp.sqrt(gmean) * root * factor[None, None]

    def finish(q):
        got = recv2[q].astype(F32)
        for h in range(2):
            c = pl.multiple_of((2 * q + h) * BLK, 128)
            scale = coef[q, h][:, 0:1]
            upd[:, pl.ds(c, WIDE)] = (got[ROWS * h : ROWS * h + ROWS] * scale).astype(BF16)
            last = [got[12 + 2 * h + r : 13 + 2 * h + r, 128 * k : 128 * k + 128] for r in range(2) for k in range(3)]
            upd[:, pl.ds(c + WIDE, 128)] = (jnp.concatenate(last, axis=0) * scale).astype(BF16)

    finish(p)
    for off in range(1, PLANE):
        second[off - 1].wait_recv()
        finish((p + PLANE - off) % PLANE)
    stores.append(pltpu.make_async_copy(upd, upd_out, sstore.at[2]))
    stores[2].start()

    for cp in second + mp_s:
        cp.wait_send()
    for cp in stores:
        cp.wait()


def place_out(upd, lnew, rnew, upd_out, lnew_out, rnew_out, upd_mid, lnew_mid, rnew_mid, sem):
    legs = ((lnew, lnew_mid, lnew_out), (rnew, rnew_mid, rnew_out), (upd, upd_mid, upd_out))
    inward = [pltpu.make_async_copy(a, b, sem.at[0, i]) for i, (a, b, _) in enumerate(legs)]
    outward = [pltpu.make_async_copy(b, c, sem.at[1, i]) for i, (_, b, c) in enumerate(legs)]
    for cp in inward:
        cp.start()
    for there, on in zip(inward, outward):
        there.wait()
        on.start()
    for cp in outward:
        cp.wait()


def on_device(gradient, left_stat, right_stat, left_root, right_root):
    hbm = pl.BlockSpec(memory_space=pltpu.HBM)
    dma = pltpu.SemaphoreType.DMA
    shapes = (
        jax.ShapeDtypeStruct((ROWS, 2 * PLANE * BLK), BF16),
        jax.ShapeDtypeStruct((QUART, BLK), F32),
        jax.ShapeDtypeStruct((QUART, BLK), F32),
    )
    update, left_new, right_new = pl.pallas_call(
        kernel,
        out_shape=shapes,
        in_specs=[hbm] * 5,
        out_specs=(hbm, hbm, hbm),
        scratch_shapes=[
            pltpu.VMEM((ROWS, 2 * PLANE * BLK), BF16),
            pltpu.VMEM((QUART, BLK), F32),
            pltpu.VMEM((QUART, BLK), F32),
            pltpu.VMEM((ROWS, 2 * PLANE * BLK), BF16),
            pltpu.VMEM((QUART, BLK), F32),
            pltpu.VMEM((QUART, BLK), F32),
            pltpu.VMEM((SUBS, PLANE, 16, PART), BF16),
            pltpu.VMEM((SUBS, PLANE, 16, PART), BF16),
            pltpu.VMEM((SUBS, RING, CHUNK, PART), BF16),
            pltpu.VMEM((SUBS, CHUNK, PART), BF16),
            pltpu.VMEM((2, SUBS, CHUNK, PART), BF16),
            pltpu.VMEM((2, QUART, BLK), BF16),
            pltpu.VMEM((2, QUART, BLK), BF16),
            pltpu.VMEM((BLK, BLK), BF16),
            pltpu.VMEM((BLK, 384), BF16),
            pltpu.VMEM((384, BLK), BF16),
            pltpu.VMEM((384, BLK), BF16),
            pltpu.VMEM((RING, CHUNK, 384), BF16),
            pltpu.VMEM((RING, 8, 128), F32),
            pltpu.VMEM((BLK, BLK), BF16),
            pltpu.VMEM((RING, 48, 384), BF16),
            pltpu.VMEM((RING, 48, 384), BF16),
            pltpu.VMEM((8, 128), F32),
            pltpu.VMEM((RING, 8, 128), F32),
            pltpu.VMEM((2, 8, 128), F32),
            pltpu.VMEM((PLANE, 2, 8, 128), F32),
            pltpu.VMEM((8, 128), F32),
            pltpu.VMEM((SLABS, 8, 128), F32),
            pltpu.VMEM((PLANE, 2, 1, 128), F32),
            pltpu.VMEM((PLANE, 16, WIDE), BF16),
            pltpu.VMEM((PLANE, 16, WIDE), BF16),
            dma((5,)),
            dma((3,)),
            dma((SUBS, PLANE)), dma((SUBS, PLANE)),
            dma((2, 6)), dma((2, 6)),
            dma((5, SUBS)), dma((6, SUBS)),
            dma((5, SUBS)), dma((6, SUBS)),
            dma((2, SUBS)), dma((2, SUBS)),
            dma((RING,)), dma((RING,)),
            dma((RING,)), dma((RING,)),
            dma((PLANE,)), dma((PLANE,)),
            dma((SLABS,)), dma((SLABS,)),
            dma((PLANE,)), dma((PLANE,)),
        ],
        compiler_params=pltpu.CompilerParams(
            collective_id=0, has_side_effects=True, vmem_limit_bytes=63 * 1024 * 1024
        ),
    )(gradient[0], left_stat[0], right_stat[0], left_root[0], right_root[0])
    update, left_new, right_new = pl.pallas_call(
        place_out,
        out_shape=shapes,
        in_specs=[hbm] * 3,
        out_specs=(hbm, hbm, hbm),
        scratch_shapes=[
            pltpu.VMEM((ROWS, 2 * PLANE * BLK), BF16),
            pltpu.VMEM((QUART, BLK), F32),
            pltpu.VMEM((QUART, BLK), F32),
            dma((2, 3)),
        ],
        compiler_params=pltpu.CompilerParams(vmem_limit_bytes=63 * 1024 * 1024),
    )(update, left_new, right_new)
    return (update[None], left_new[None], right_new[None])


def solution(mesh):
    spec = P("mp", "dp", None)
    return jax.shard_map(
        on_device, mesh=mesh, in_specs=(spec,) * 5, out_specs=(spec,) * 3, check_vma=False
    )
```

```python
import functools

import jax
import jax.numpy as jnp
from jax import lax
from jax.experimental import pallas as pl
from jax.experimental.pallas import tpu as pltpu
from jax.sharding import PartitionSpec as P

MESH = pl.DeviceIdType.MESH
F32 = jnp.float32
BF16 = jnp.bfloat16

BLK = 768
PLANE = 16
RING = 8
SLABS = 6
ROWS = 6
QUART = 192
PARTS = 4
WIDE = 640
SUBS = 2
CHUNK = PLANE * ROWS
PART = BLK // SUBS

stat_decay = 0.9999
epsilon = 1e-06
clip_rms = 1.0


def iota(shape, dim):
    return lax.broadcasted_iota(jnp.int32, shape, dim)


def by6(v):
    q = (v * 10923) >> 16
    return q, v - q * 6


def one_hot(rows, cols, target):
    return jnp.where(iota((rows, cols), 0) == target(iota((rows, cols), 1)), 1.0, 0.0).astype(BF16)


def dot(a, b):
    return jnp.dot(a, b, preferred_element_type=F32)


def dot_nt(a, b):
    return lax.dot_general(a, b, (((1,), (1,)), ((), ())), preferred_element_type=F32)


def column_part(i):
    size = 2 * PLANE * BLK // PARTS
    return pl.ds(i * size, size)


def row_part(i):
    return pl.ds(i * (QUART // PARTS), QUART // PARTS)


def kernel(
    grad, lstat, rstat, lroot, rroot, upd_out, lnew_out, rnew_out,
    upd, lnew, rnew, gin, lold, rold, gsend, recv1, gfull, obuf, tbuf, rrp, lrp, order, cols, leftp, leftq, mixed, gsq, gtrue, ubuf, recvu,
    stat, recvs, msg, recvp, tot, recvt, coef, send2, recv2,
    sload, sgrad, sstore, s1, r1, sx, rx, sr, rr, sl, rl, st, rt, su, ru, ss, rs, sp, rp, sm, rm, s2, r2,
):
    me = lax.axis_index("dp")
    mp = lax.axis_index("mp")
    p = me // RING
    y = me % RING
    lane = y % 4
    half = y // 4
    parity = y % 2
    upper = lane // 2

    def plane_id(off):
        t = (p + off) % PLANE
        return t, (t * RING + y, mp)

    def ring_id(off):
        t = (y + off) % RING
        return t, (p * RING + t, mp)

    def mp_id(off):
        return (me, (mp + off) % SLABS)

    def remote(src, dst, send, recv, where):
        return pltpu.make_async_remote_copy(
            src_ref=src, dst_ref=dst, send_sem=send, recv_sem=recv, device_id=where, device_id_type=MESH
        )

    loads = [
        pltpu.make_async_copy(src, dst, sload.at[i])
        for i, (src, dst) in enumerate(
            ((None, None), (rroot, rrp.at[parity]), (lroot, lrp.at[upper]), (lstat, lold), (rstat, rold))
        )
        if i
    ]
    loads = [None] + loads
    pieces = [
        pltpu.make_async_copy(grad.at[:, column_part(i)], gin.at[:, column_part(i)], sgrad.at[i]) for i in range(PARTS)
    ]
    for cp in pieces:
        cp.start()
    barrier = pltpu.get_barrier_semaphore()
    peers = [plane_id(o)[1] for o in range(1, PLANE)]
    peers += [ring_id(o)[1] for o in range(1, RING)]
    peers += [mp_id(o) for o in range(1, SLABS)]
    for where in peers:
        pl.semaphore_signal(barrier, inc=1, device_id=where, device_id_type=MESH)

    for cp in loads[1:]:
        cp.start()
    gsend[...] = jnp.zeros_like(gsend)
    pl.semaphore_wait(barrier, len(peers))

    def outside(q):
        return (q * QUART + 127) // 128

    def lanes128(k):
        return pl.ds(pl.multiple_of(k * 128, 128), 128)

    def root_copies(kind, src, dst, slot, shift):
        copies = []
        for i in range(1, 6):
            part = lanes128((outside(lane + shift) + i) % 6)
            cp = remote(
                src.at[:, part], dst.at[slot, :, part], sx.at[kind, i], rx.at[kind, i], (me + shift, mp)
            )
            cp.start()
            copies.append(cp)
        return copies

    shift_r, shift_l = 1 - 2 * parity, 2 - 4 * upper
    xr = root_copies(0, rroot, rrp, parity, shift_r)
    xl = root_copies(1, lroot, lrp, upper, shift_l)

    def fill(ref, slot, shift):
        own = outside(lane)
        pick = jnp.where(iota((QUART, BLK), 1) == iota((QUART, BLK), 0) + (lane + shift) * QUART, 1.0, 0.0)
        mine = ref[slot, pl.ds(pl.multiple_of(own * 128 - lane * QUART, 64), 128), :]
        ref[1 - slot, :, lanes128(own)] = dot_nt(pick.astype(BF16), mine).astype(BF16)

    for cp in pieces:
        cp.wait()
    first = []
    for sub in range(SUBS):
        for q in range(PLANE):
            for h in range(2):
                c = (2 * q + h) * BLK + sub * PART
                gsend[sub, q, 8 * h : 8 * h + ROWS, :] = gin[:, c : c + PART]
        copies = []
        for off in range(1, PLANE):
            t, where = plane_id(off)
            cp = remote(gsend.at[sub, t], recv1.at[sub, p], s1.at[sub, off], r1.at[sub, off], where)
            cp.start()
            copies.append(cp)
        first.append(copies)
        recv1[sub, p] = gsend[sub, p]

    def compact(c):
        i = c & 7
        h = (c >> 3) & 1
        row = jnp.where(h == half, 0, CHUNK) + (c >> 4) * ROWS + i
        return jnp.where(i < ROWS, row, -1)

    def ordered(c):
        q = c >> 5
        yy = (q * 21846) >> 16
        pp, i = by6(c - yy * CHUNK)
        return pp * (RING * ROWS) + yy * ROWS + i

    def by_ring(c):
        s = (c >= QUART).astype(jnp.int32)
        q = ((c >> 4) * 21846) >> 16
        xx = q - 4 * s
        yy, i = by6(c - q * 48)
        return yy * 48 + s * 24 + xx * ROWS + i

    def spread(c):
        h = (c >= 48).astype(jnp.int32)
        q, i = by6(c - 48 * h)
        return q * 16 + h * ROWS + i

    def spread_last(block):
        def row(c):
            h = (c >= 48).astype(jnp.int32)
            q, i = by6(c - 48 * h)
            low = (i >= 3).astype(jnp.int32)
            return jnp.where(i - 3 * low == block, q * 16 + 12 + 2 * h + low, -1)

        return row

    order[...] = one_hot(BLK, BLK, ordered)
    compactor = one_hot(2 * CHUNK, PLANE * 16, compact)
    def hop(way, dist, sub, src):
        step = 1 if way == 0 else RING - 1
        slot = (y + (RING - step) * dist) % RING
        send, recv = (sr, rr) if way == 0 else (sl, rl)
        where = ring_id(step)[1]
        dst = gfull.at[sub, slot]
        return remote(dst if src is None else src, dst, send.at[dist, sub], recv.at[dist + 1, sub], where)

    def transit(way, sub):
        step = 1 if way == 0 else RING - 1
        return remote(
            obuf.at[sub], tbuf.at[way, sub], st.at[way, sub], rt.at[way, sub], ring_id(step)[1]
        )

    def slot_of(way, dist):
        return (y + (RING - 1 if way == 0 else 1) * dist) % RING

    def arrival(way, dist, sub):
        recv = rr if way == 0 else rl
        slot = slot_of(way, dist)
        where = ring_id(1 if way == 0 else RING - 1)[1]
        there = gfull.at[sub, slot]
        remote(there, there, recv.at[dist, sub], recv.at[dist, sub], where).wait_recv()

    def multiply(slot):
        total, squares = 0.0, 0.0
        for sub in range(SUBS):
            chunk = gfull[sub, slot]
            total = total + dot(chunk, cols[PART * sub : PART * sub + PART])
            squares = squares + jnp.sum(jnp.square(chunk.astype(F32)), keepdims=True)
        mixed[slot] = total.astype(BF16)
        gsq[slot] = jnp.broadcast_to(squares, (8, 128))

    ranks = (lane, 3 - lane)
    for sub in range(SUBS):
        for cp in first[sub]:
            cp.wait_recv()
        packed = dot(compactor, recv1[sub].reshape(PLANE * 16, PART)).astype(BF16)
        gfull[sub, y] = packed[:CHUNK]
        obuf[sub] = packed[CHUNK:]
        for way in range(2):

            @pl.when(ranks[way] == 2)
            def _():
                transit(way, sub).start()

        for way in range(2):

            @pl.when(ranks[way] <= 2)
            def _():
                hop(way, 0, sub, None).start()

            @pl.when(ranks[way] == 3)
            def _():
                hop(way, 0, sub, obuf.at[sub]).start()

    for dist in range(1, 6):
        for sub in range(SUBS):
            for way in range(2):
                rank = ranks[way]
                if dist == 1:

                    @pl.when(rank == 3)
                    def _():
                        transit(way, sub).wait_recv()
                        hop(way, 1, sub, tbuf.at[way, sub]).start()

                @pl.when(dist <= rank + 2)
                def _():
                    arrival(way, dist, sub)
                    if dist <= 4:

                        @pl.when(rank <= 2)
                        def _():
                            hop(way, dist, sub, None).start()

        if dist == 3:
            loads[1].wait()
            loads[2].wait()
            for cp in xr:
                cp.wait_recv()
            fill(rrp, parity, shift_r)
            cols[...] = jnp.transpose(rrp[...].reshape(384, BLK))
            for cp in xl:
                cp.wait_recv()
            fill(lrp, upper, shift_l)
            left_rows = dot(one_hot(384, 384, by_ring), lrp[...].reshape(384, BLK)).astype(BF16)
            leftp[...] = left_rows
        if dist < 4:
            continue
        if dist == 4:
            leftq[...] = dot(leftp[...], order[...]).astype(BF16)
            multiply(y)
        for back in (1, 2, 3, 4) if dist == 4 else (dist,):
            for way in range(2):

                @pl.when(back <= ranks[way] + 2)
                def _():
                    multiply(slot_of(way, back))

    direction = dot(leftq[...], mixed[...].reshape(BLK, 384))
    partial = jnp.sum(jnp.square(direction), keepdims=True)
    stat[...] = jnp.where(iota((8, 128), 0) == 0, partial, jnp.sum(gsq[...], axis=0) * 0.25)
    ring_s = []
    for off in range(1, RING):
        t, where = ring_id(off)
        cs = remote(stat, recvs.at[y], ss.at[off], rs.at[off], where)
        cs.start()
        ring_s.append(cs)
    ubuf[...] = direction.astype(BF16).reshape(RING, 48, 384)
    ring_u = []
    for off in (4, 2, 6, 3, 5, 1, 7):
        t, where = ring_id(off)
        cu = remote(ubuf.at[t], recvu.at[y], su.at[off], ru.at[off], where)
        cu.start()
        ring_u.append(cu)
    recvs[y] = stat[...]
    recvu[y] = ubuf[y]

    def reorder(k):
        for sub in range(SUBS):
            gtrue[QUART * k : QUART * k + QUART, PART * sub : PART * sub + PART] = dot(
                order[QUART * k : QUART * k + QUART], gfull[sub].reshape(BLK, PART)
            ).astype(BF16)

    reorder(0)
    reorder(1)

    for cs in ring_s:
        cs.wait_recv()
    for h in range(2):
        msg[h] = recvs[4 * h] + recvs[4 * h + 1] + recvs[4 * h + 2] + recvs[4 * h + 3]
    plane_s = []
    for off in range(1, PLANE):
        t, where = plane_id(off)
        cp = remote(msg, recvp.at[p], sp.at[off], rp.at[off], where)
        cp.start()
        plane_s.append(cp)
    recvp[p] = msg[...]
    reorder(2)
    reorder(3)

    loads[3].wait()
    loads[4].wait()
    rows = gtrue[pl.ds(pl.multiple_of(lane * QUART, QUART), QUART), :]
    lnew[...] = stat_decay * lold[...] + (1.0 - stat_decay) * dot_nt(rows, gtrue[...])
    stores = [pltpu.make_async_copy(lnew, lnew_out, sstore.at[0])]
    stores[0].start()
    pick = jnp.where(iota((QUART, BLK), 1) == iota((QUART, BLK), 0) + lane * QUART, 1.0, 0.0).astype(BF16)
    columns = dot_nt(pick, gtrue[...]).astype(BF16)
    rnew[...] = stat_decay * rold[...] + (1.0 - stat_decay) * dot(columns, gtrue[...])
    stores.append(pltpu.make_async_copy(rnew, rnew_out, sstore.at[1]))
    stores[1].start()

    for cp in first[0] + first[1] + xr + xl:
        cp.wait_send()
    for way in range(2):
        rank = ranks[way]

        @pl.when(rank == 2)
        def _():
            for sub in range(SUBS):
                transit(way, sub).wait_send()

        for dist in range(5):
            count = jnp.where(rank == 3, 2, rank + 3)

            @pl.when(dist < count)
            def _():
                for sub in range(SUBS):
                    hop(way, dist, sub, None).wait_send()

    place = one_hot(128, 96, spread)
    place_last = [one_hot(128, 96, spread_last(block)) for block in range(3)]
    second = []
    for off in range(1, PLANE):
        t, where = plane_id(off)
        second.append(remote(send2.at[t], recv2.at[p], s2.at[off], r2.at[off], where))

    for group in range(2):
        e = (parity + group) % 2
        for cu in ring_u[:3] if group == 0 else ring_u[3:]:
            cu.wait_recv()
        both = [jnp.concatenate([recvu[2 * k + e], recvu[4 + 2 * k + e]], axis=0) for k in range(2)]
        both = jnp.concatenate(both, axis=1)
        last = jnp.concatenate([dot(at, both[:, WIDE:]) for at in place_last], axis=1)
        out = dot(place, both[:, :WIDE])
        out = jnp.concatenate([out[:, :384] + last, out[:, 384:]], axis=1).astype(BF16)
        for s in range(2):
            for xx in range(4):
                send2[(e + 2 * s) * 4 + xx] = out[(4 * s + xx) * 16 : (4 * s + xx) * 16 + 16]
        z, x = p // 4, p % 4
        for s in (1, 0):
            for dx in (2, 1, 3, 0):
                t = (z + (e + z) % 2 + 2 * s) % 4 * 4 + (x + dx) % 4
                off = (t + PLANE - p) % PLANE

                @pl.when(off > 0)
                def _():
                    remote(send2.at[t], recv2.at[p], s2.at[off], r2.at[off], (t * RING + y, mp)).start()

    for cp in plane_s:
        cp.wait_recv()
    size = float(BLK * BLK)
    square = recvp[:, :, 0:1, :] * (1.0 / size)
    gmean = recvp[:, :, 1:2, :] * (1.0 / size)
    root = lax.rsqrt(square + epsilon)
    slab = jnp.sum(gmean * square * root * root, axis=(0, 1))
    tot[...] = jnp.broadcast_to(slab, (8, 128))
    mp_s = []
    for off in range(1, SLABS):
        cp = remote(tot, recvt.at[mp], sm.at[off], rm.at[off], mp_id(off))
        cp.start()
        mp_s.append(cp)
    recvt[mp] = tot[...]
    recv2[p] = send2[p]

    for cp in ring_s + ring_u + plane_s:
        cp.wait_send()
    for cp in mp_s:
        cp.wait_recv()
    total = jnp.sum(recvt[...], axis=0)[0:1] * (1.0 / float(2 * PLANE * SLABS))
    factor = jnp.minimum(1.0, clip_rms * lax.rsqrt(total + epsilon))
    coef[...] = jnp.sqrt(gmean) * root * factor[None, None]

    def finish(q):
        got = recv2[q].astype(F32)
        for h in range(2):
            c = pl.multiple_of((2 * q + h) * BLK, 128)
            scale = coef[q, h][:, 0:1]
            upd[:, pl.ds(c, WIDE)] = (got[ROWS * h : ROWS * h + ROWS] * scale).astype(BF16)
            last = [got[12 + 2 * h + r : 13 + 2 * h + r, 128 * k : 128 * k + 128] for r in range(2) for k in range(3)]
            upd[:, pl.ds(c + WIDE, 128)] = (jnp.concatenate(last, axis=0) * scale).astype(BF16)

    finish(p)
    for off in range(1, PLANE):
        second[off - 1].wait_recv()
        finish((p + PLANE - off) % PLANE)
    for i in range(PARTS):
        stores.append(
            pltpu.make_async_copy(upd.at[:, column_part(i)], upd_out.at[:, column_part(i)], sstore.at[2 + i])
        )
        stores[2 + i].start()

    for cp in second + mp_s:
        cp.wait_send()
    for cp in stores:
        cp.wait()


def place_out(upd, lnew, rnew, upd_out, lnew_out, rnew_out, upd_mid, lnew_mid, rnew_mid, sem):
    legs = []
    for i in range(PARTS):
        r, c = row_part(i), column_part(i)
        legs.append((lnew.at[r], lnew_mid.at[r], lnew_out.at[r]))
        legs.append((rnew.at[r], rnew_mid.at[r], rnew_out.at[r]))
        legs.append((upd.at[:, c], upd_mid.at[:, c], upd_out.at[:, c]))
    inward = [pltpu.make_async_copy(a, b, sem.at[0, i]) for i, (a, b, _) in enumerate(legs)]
    outward = [pltpu.make_async_copy(b, c, sem.at[1, i]) for i, (_, b, c) in enumerate(legs)]
    for cp in inward:
        cp.start()
    for there, on in zip(inward, outward):
        there.wait()
        on.start()
    for cp in outward:
        cp.wait()


def on_device(gradient, left_stat, right_stat, left_root, right_root):
    hbm = pl.BlockSpec(memory_space=pltpu.HBM)
    dma = pltpu.SemaphoreType.DMA
    shapes = (
        jax.ShapeDtypeStruct((ROWS, 2 * PLANE * BLK), BF16),
        jax.ShapeDtypeStruct((QUART, BLK), F32),
        jax.ShapeDtypeStruct((QUART, BLK), F32),
    )
    update, left_new, right_new = pl.pallas_call(
        kernel,
        out_shape=shapes,
        in_specs=[hbm] * 5,
        out_specs=(hbm, hbm, hbm),
        scratch_shapes=[
            pltpu.VMEM((ROWS, 2 * PLANE * BLK), BF16),
            pltpu.VMEM((QUART, BLK), F32),
            pltpu.VMEM((QUART, BLK), F32),
            pltpu.VMEM((ROWS, 2 * PLANE * BLK), BF16),
            pltpu.VMEM((QUART, BLK), F32),
            pltpu.VMEM((QUART, BLK), F32),
            pltpu.VMEM((SUBS, PLANE, 16, PART), BF16),
            pltpu.VMEM((SUBS, PLANE, 16, PART), BF16),
            pltpu.VMEM((SUBS, RING, CHUNK, PART), BF16),
            pltpu.VMEM((SUBS, CHUNK, PART), BF16),
            pltpu.VMEM((2, SUBS, CHUNK, PART), BF16),
            pltpu.VMEM((2, QUART, BLK), BF16),
            pltpu.VMEM((2, QUART, BLK), BF16),
            pltpu.VMEM((BLK, BLK), BF16),
            pltpu.VMEM((BLK, 384), BF16),
            pltpu.VMEM((384, BLK), BF16),
            pltpu.VMEM((384, BLK), BF16),
            pltpu.VMEM((RING, CHUNK, 384), BF16),
            pltpu.VMEM((RING, 8, 128), F32),
            pltpu.VMEM((BLK, BLK), BF16),
            pltpu.VMEM((RING, 48, 384), BF16),
            pltpu.VMEM((RING, 48, 384), BF16),
            pltpu.VMEM((8, 128), F32),
            pltpu.VMEM((RING, 8, 128), F32),
            pltpu.VMEM((2, 8, 128), F32),
            pltpu.VMEM((PLANE, 2, 8, 128), F32),
            pltpu.VMEM((8, 128), F32),
            pltpu.VMEM((SLABS, 8, 128), F32),
            pltpu.VMEM((PLANE, 2, 1, 128), F32),
            pltpu.VMEM((PLANE, 16, WIDE), BF16),
            pltpu.VMEM((PLANE, 16, WIDE), BF16),
            dma((5,)),
            dma((PARTS,)),
            dma((2 + PARTS,)),
            dma((SUBS, PLANE)), dma((SUBS, PLANE)),
            dma((2, 6)), dma((2, 6)),
            dma((5, SUBS)), dma((6, SUBS)),
            dma((5, SUBS)), dma((6, SUBS)),
            dma((2, SUBS)), dma((2, SUBS)),
            dma((RING,)), dma((RING,)),
            dma((RING,)), dma((RING,)),
            dma((PLANE,)), dma((PLANE,)),
            dma((SLABS,)), dma((SLABS,)),
            dma((PLANE,)), dma((PLANE,)),
        ],
        compiler_params=pltpu.CompilerParams(
            collective_id=0, has_side_effects=True, vmem_limit_bytes=63 * 1024 * 1024
        ),
    )(gradient[0], left_stat[0], right_stat[0], left_root[0], right_root[0])
    update, left_new, right_new = pl.pallas_call(
        place_out,
        out_shape=shapes,
        in_specs=[hbm] * 3,
        out_specs=(hbm, hbm, hbm),
        scratch_shapes=[
            pltpu.VMEM((ROWS, 2 * PLANE * BLK), BF16),
            pltpu.VMEM((QUART, BLK), F32),
            pltpu.VMEM((QUART, BLK), F32),
            dma((2, 3 * PARTS)),
        ],
        compiler_params=pltpu.CompilerParams(vmem_limit_bytes=63 * 1024 * 1024),
    )(update, left_new, right_new)
    return (update[None], left_new[None], right_new[None])


def solution(mesh):
    spec = P("mp", "dp", None)
    return jax.shard_map(
        on_device, mesh=mesh, in_specs=(spec,) * 5, out_specs=(spec,) * 3, check_vma=False
    )
```

```python
import functools

import jax
import jax.numpy as jnp
from jax import lax
from jax.experimental import pallas as pl
from jax.experimental.pallas import tpu as pltpu
from jax.sharding import PartitionSpec as P

MESH = pl.DeviceIdType.MESH
F32 = jnp.float32
BF16 = jnp.bfloat16

BLK = 768
PLANE = 16
RING = 8
SLABS = 6
ROWS = 6
QUART = 192
WIDE = 640
SUBS = 2
CHUNK = PLANE * ROWS
PART = BLK // SUBS

stat_decay = 0.9999
epsilon = 1e-06
clip_rms = 1.0


def iota(shape, dim):
    return lax.broadcasted_iota(jnp.int32, shape, dim)


def by6(v):
    q = (v * 10923) >> 16
    return q, v - q * 6


def one_hot(rows, cols, target):
    return jnp.where(iota((rows, cols), 0) == target(iota((rows, cols), 1)), 1.0, 0.0).astype(BF16)


def dot(a, b):
    return jnp.dot(a, b, preferred_element_type=F32)


def dot_nt(a, b):
    return lax.dot_general(a, b, (((1,), (1,)), ((), ())), preferred_element_type=F32)


def kernel(
    grad, lstat, rstat, lroot, rroot, upd_out, lnew_out, rnew_out,
    upd, lnew, rnew, gin, lold, rold, gsend, recv1, gfull, obuf, tbuf, rrp, lrp, order, cols, leftp, leftq, mixed, gsq, gtrue, ubuf, recvu,
    stat, recvs, msg, recvp, tot, recvt, coef, send2, recv2,
    sload, sstore, s1, r1, sx, rx, sr, rr, sl, rl, st, rt, su, ru, ss, rs, sp, rp, sm, rm, s2, r2,
):
    me = lax.axis_index("dp")
    mp = lax.axis_index("mp")
    p = me // RING
    y = me % RING
    lane = y % 4
    half = y // 4
    parity = y % 2
    upper = lane // 2

    def plane_id(off):
        t = (p + off) % PLANE
        return t, (t * RING + y, mp)

    def ring_id(off):
        t = (y + off) % RING
        return t, (p * RING + t, mp)

    def mp_id(off):
        return (me, (mp + off) % SLABS)

    def remote(src, dst, send, recv, where):
        return pltpu.make_async_remote_copy(
            src_ref=src, dst_ref=dst, send_sem=send, recv_sem=recv, device_id=where, device_id_type=MESH
        )

    loads = [
        pltpu.make_async_copy(src, dst, sload.at[i])
        for i, (src, dst) in enumerate(
            ((grad, gin), (rroot, rrp.at[parity]), (lroot, lrp.at[upper]), (lstat, lold), (rstat, rold))
        )
    ]
    loads[0].start()
    barrier = pltpu.get_barrier_semaphore()
    peers = [plane_id(o)[1] for o in range(1, PLANE)]
    peers += [ring_id(o)[1] for o in range(1, RING)]
    peers += [mp_id(o) for o in range(1, SLABS)]
    for where in peers:
        pl.semaphore_signal(barrier, inc=1, device_id=where, device_id_type=MESH)

    for cp in loads[1:]:
        cp.start()
    gsend[...] = jnp.zeros_like(gsend)
    pl.semaphore_wait(barrier, len(peers))

    def outside(q):
        return (q * QUART + 127) // 128

    def lanes128(k):
        return pl.ds(pl.multiple_of(k * 128, 128), 128)

    def root_copies(kind, src, dst, slot, shift):
        copies = []
        for i in range(1, 6):
            part = lanes128((outside(lane + shift) + i) % 6)
            cp = remote(
                src.at[:, part], dst.at[slot, :, part], sx.at[kind, i], rx.at[kind, i], (me + shift, mp)
            )
            cp.start()
            copies.append(cp)
        return copies

    shift_r, shift_l = 1 - 2 * parity, 2 - 4 * upper

    def fill(ref, slot, shift):
        own = outside(lane)
        pick = jnp.where(iota((QUART, BLK), 1) == iota((QUART, BLK), 0) + (lane + shift) * QUART, 1.0, 0.0)
        mine = ref[slot, pl.ds(pl.multiple_of(own * 128 - lane * QUART, 64), 128), :]
        ref[1 - slot, :, lanes128(own)] = dot_nt(pick.astype(BF16), mine).astype(BF16)

    loads[0].wait()
    first = []
    for sub in range(SUBS):
        for q in range(PLANE):
            for h in range(2):
                c = (2 * q + h) * BLK + sub * PART
                gsend[sub, q, 8 * h : 8 * h + ROWS, :] = gin[:, c : c + PART]
        copies = []
        for off in range(1, PLANE):
            t, where = plane_id(off)
            cp = remote(gsend.at[sub, t], recv1.at[sub, p], s1.at[sub, off], r1.at[sub, off], where)
            cp.start()
            copies.append(cp)
        first.append(copies)
        if sub == 0:
            xr = root_copies(0, rroot, rrp, parity, shift_r)
            xl = root_copies(1, lroot, lrp, upper, shift_l)
        recv1[sub, p] = gsend[sub, p]

    def compact(c):
        i = c & 7
        h = (c >> 3) & 1
        row = jnp.where(h == half, 0, CHUNK) + (c >> 4) * ROWS + i
        return jnp.where(i < ROWS, row, -1)

    def ordered(c):
        q = c >> 5
        yy = (q * 21846) >> 16
        pp, i = by6(c - yy * CHUNK)
        return pp * (RING * ROWS) + yy * ROWS + i

    def by_ring(c):
        s = (c >= QUART).astype(jnp.int32)
        q = ((c >> 4) * 21846) >> 16
        xx = q - 4 * s
        yy, i = by6(c - q * 48)
        return yy * 48 + s * 24 + xx * ROWS + i

    def spread(c):
        h = (c >= 48).astype(jnp.int32)
        q, i = by6(c - 48 * h)
        return q * 16 + h * ROWS + i

    def spread_last(block):
        def row(c):
            h = (c >= 48).astype(jnp.int32)
            q, i = by6(c - 48 * h)
            low = (i >= 3).astype(jnp.int32)
            return jnp.where(i - 3 * low == block, q * 16 + 12 + 2 * h + low, -1)

        return row

    order[...] = one_hot(BLK, BLK, ordered)
    compactor = one_hot(2 * CHUNK, PLANE * 16, compact)
    def hop(way, dist, sub, src):
        step = 1 if way == 0 else RING - 1
        slot = (y + (RING - step) * dist) % RING
        send, recv = (sr, rr) if way == 0 else (sl, rl)
        where = ring_id(step)[1]
        dst = gfull.at[sub, slot]
        return remote(dst if src is None else src, dst, send.at[dist, sub], recv.at[dist + 1, sub], where)

    def transit(way, sub):
        step = 1 if way == 0 else RING - 1
        return remote(
            obuf.at[sub], tbuf.at[way, sub], st.at[way, sub], rt.at[way, sub], ring_id(step)[1]
        )

    def slot_of(way, dist):
        return (y + (RING - 1 if way == 0 else 1) * dist) % RING

    def arrival(way, dist, sub):
        recv = rr if way == 0 else rl
        slot = slot_of(way, dist)
        where = ring_id(1 if way == 0 else RING - 1)[1]
        there = gfull.at[sub, slot]
        remote(there, there, recv.at[dist, sub], recv.at[dist, sub], where).wait_recv()

    def multiply(slot):
        total, squares = 0.0, 0.0
        for sub in range(SUBS):
            chunk = gfull[sub, slot]
            total = total + dot(chunk, cols[PART * sub : PART * sub + PART])
            squares = squares + jnp.sum(jnp.square(chunk.astype(F32)), keepdims=True)
        mixed[slot] = total.astype(BF16)
        gsq[slot] = jnp.broadcast_to(squares, (8, 128))

    ranks = (lane, 3 - lane)
    for sub in range(SUBS):
        for cp in first[sub]:
            cp.wait_recv()
        packed = dot(compactor, recv1[sub].reshape(PLANE * 16, PART)).astype(BF16)
        gfull[sub, y] = packed[:CHUNK]
        obuf[sub] = packed[CHUNK:]
        for way in range(2):

            @pl.when(ranks[way] == 2)
            def _():
                transit(way, sub).start()

        for way in range(2):

            @pl.when(ranks[way] <= 2)
            def _():
                hop(way, 0, sub, None).start()

            @pl.when(ranks[way] == 3)
            def _():
                hop(way, 0, sub, obuf.at[sub]).start()

    for dist in range(1, 6):
        for sub in range(SUBS):
            for way in range(2):
                rank = ranks[way]
                if dist == 1:

                    @pl.when(rank == 3)
                    def _():
                        transit(way, sub).wait_recv()
                        hop(way, 1, sub, tbuf.at[way, sub]).start()

                @pl.when(dist <= rank + 2)
                def _():
                    arrival(way, dist, sub)
                    if dist <= 4:

                        @pl.when(rank <= 2)
                        def _():
                            hop(way, dist, sub, None).start()

        if dist == 3:
            loads[1].wait()
            loads[2].wait()
            for cp in xr:
                cp.wait_recv()
            fill(rrp, parity, shift_r)
            cols[...] = jnp.transpose(rrp[...].reshape(384, BLK))
            for cp in xl:
                cp.wait_recv()
            fill(lrp, upper, shift_l)
            left_rows = dot(one_hot(384, 384, by_ring), lrp[...].reshape(384, BLK)).astype(BF16)
            leftp[...] = left_rows
        if dist < 4:
            continue
        if dist == 4:
            leftq[...] = dot(leftp[...], order[...]).astype(BF16)
            multiply(y)
        for back in (1, 2, 3, 4) if dist == 4 else (dist,):
            for way in range(2):

                @pl.when(back <= ranks[way] + 2)
                def _():
                    multiply(slot_of(way, back))

    direction = dot(leftq[...], mixed[...].reshape(BLK, 384))
    partial = jnp.sum(jnp.square(direction), keepdims=True)
    stat[...] = jnp.where(iota((8, 128), 0) == 0, partial, jnp.sum(gsq[...], axis=0) * 0.25)
    ring_s = []
    for off in range(1, RING):
        t, where = ring_id(off)
        cs = remote(stat, recvs.at[y], ss.at[off], rs.at[off], where)
        cs.start()
        ring_s.append(cs)
    ubuf[...] = direction.astype(BF16).reshape(RING, 48, 384)
    ring_u = []
    for off in (4, 2, 6, 3, 5, 1, 7):
        t, where = ring_id(off)
        cu = remote(ubuf.at[t], recvu.at[y], su.at[off], ru.at[off], where)
        cu.start()
        ring_u.append(cu)
    recvs[y] = stat[...]
    recvu[y] = ubuf[y]

    def reorder(k):
        for sub in range(SUBS):
            gtrue[QUART * k : QUART * k + QUART, PART * sub : PART * sub + PART] = dot(
                order[QUART * k : QUART * k + QUART], gfull[sub].reshape(BLK, PART)
            ).astype(BF16)

    reorder(0)
    reorder(1)

    for cs in ring_s:
        cs.wait_recv()
    for h in range(2):
        msg[h] = recvs[4 * h] + recvs[4 * h + 1] + recvs[4 * h + 2] + recvs[4 * h + 3]
    plane_s = []
    for off in range(1, PLANE):
        t, where = plane_id(off)
        cp = remote(msg, recvp.at[p], sp.at[off], rp.at[off], where)
        cp.start()
        plane_s.append(cp)
    recvp[p] = msg[...]
    reorder(2)
    reorder(3)

    loads[3].wait()
    loads[4].wait()
    rows = gtrue[pl.ds(pl.multiple_of(lane * QUART, QUART), QUART), :]
    lnew[...] = stat_decay * lold[...] + (1.0 - stat_decay) * dot_nt(rows, gtrue[...])
    stores = [pltpu.make_async_copy(lnew, lnew_out, sstore.at[0])]
    stores[0].start()
    pick = jnp.where(iota((QUART, BLK), 1) == iota((QUART, BLK), 0) + lane * QUART, 1.0, 0.0).astype(BF16)
    columns = dot_nt(pick, gtrue[...]).astype(BF16)
    rnew[...] = stat_decay * rold[...] + (1.0 - stat_decay) * dot(columns, gtrue[...])
    stores.append(pltpu.make_async_copy(rnew, rnew_out, sstore.at[1]))
    stores[1].start()

    for cp in first[0] + first[1] + xr + xl:
        cp.wait_send()
    for way in range(2):
        rank = ranks[way]

        @pl.when(rank == 2)
        def _():
            for sub in range(SUBS):
                transit(way, sub).wait_send()

        for dist in range(5):
            count = jnp.where(rank == 3, 2, rank + 3)

            @pl.when(dist < count)
            def _():
                for sub in range(SUBS):
                    hop(way, dist, sub, None).wait_send()

    place = one_hot(128, 96, spread)
    place_last = [one_hot(128, 96, spread_last(block)) for block in range(3)]
    second = []
    for off in range(1, PLANE):
        t, where = plane_id(off)
        second.append(remote(send2.at[t], recv2.at[p], s2.at[off], r2.at[off], where))

    for group in range(2):
        e = (parity + group) % 2
        for cu in ring_u[:3] if group == 0 else ring_u[3:]:
            cu.wait_recv()
        both = [jnp.concatenate([recvu[2 * k + e], recvu[4 + 2 * k + e]], axis=0) for k in range(2)]
        both = jnp.concatenate(both, axis=1)
        last = jnp.concatenate([dot(at, both[:, WIDE:]) for at in place_last], axis=1)
        out = dot(place, both[:, :WIDE])
        out = jnp.concatenate([out[:, :384] + last, out[:, 384:]], axis=1).astype(BF16)
        for s in range(2):
            for xx in range(4):
                send2[(e + 2 * s) * 4 + xx] = out[(4 * s + xx) * 16 : (4 * s + xx) * 16 + 16]
        z, x = p // 4, p % 4
        for s in (1, 0):
            for dx in (2, 1, 3, 0):
                t = (z + (e + z) % 2 + 2 * s) % 4 * 4 + (x + dx) % 4
                off = (t + PLANE - p) % PLANE

                @pl.when(off > 0)
                def _():
                    remote(send2.at[t], recv2.at[p], s2.at[off], r2.at[off], (t * RING + y, mp)).start()

    for cp in plane_s:
        cp.wait_recv()
    size = float(BLK * BLK)
    square = recvp[:, :, 0:1, :] * (1.0 / size)
    gmean = recvp[:, :, 1:2, :] * (1.0 / size)
    root = lax.rsqrt(square + epsilon)
    slab = jnp.sum(gmean * square * root * root, axis=(0, 1))
    tot[...] = jnp.broadcast_to(slab, (8, 128))
    mp_s = []
    for off in range(1, SLABS):
        cp = remote(tot, recvt.at[mp], sm.at[off], rm.at[off], mp_id(off))
        cp.start()
        mp_s.append(cp)
    recvt[mp] = tot[...]
    recv2[p] = send2[p]

    for cp in ring_s + ring_u + plane_s:
        cp.wait_send()
    for cp in mp_s:
        cp.wait_recv()
    total = jnp.sum(recvt[...], axis=0)[0:1] * (1.0 / float(2 * PLANE * SLABS))
    factor = jnp.minimum(1.0, clip_rms * lax.rsqrt(total + epsilon))
    coef[...] = jnp.sqrt(gmean) * root * factor[None, None]

    def finish(q):
        got = recv2[q].astype(F32)
        for h in range(2):
            c = pl.multiple_of((2 * q + h) * BLK, 128)
            scale = coef[q, h][:, 0:1]
            upd[:, pl.ds(c, WIDE)] = (got[ROWS * h : ROWS * h + ROWS] * scale).astype(BF16)
            last = [got[12 + 2 * h + r : 13 + 2 * h + r, 128 * k : 128 * k + 128] for r in range(2) for k in range(3)]
            upd[:, pl.ds(c + WIDE, 128)] = (jnp.concatenate(last, axis=0) * scale).astype(BF16)

    finish(p)
    for off in range(1, PLANE):
        second[off - 1].wait_recv()
        finish((p + PLANE - off) % PLANE)
    stores.append(pltpu.make_async_copy(upd, upd_out, sstore.at[2]))
    stores[2].start()

    for cp in second + mp_s:
        cp.wait_send()
    for cp in stores:
        cp.wait()


def place_out(upd, lnew, rnew, upd_out, lnew_out, rnew_out, upd_mid, lnew_mid, rnew_mid, sem):
    legs = ((lnew, lnew_mid, lnew_out), (rnew, rnew_mid, rnew_out), (upd, upd_mid, upd_out))
    inward = [pltpu.make_async_copy(a, b, sem.at[0, i]) for i, (a, b, _) in enumerate(legs)]
    outward = [pltpu.make_async_copy(b, c, sem.at[1, i]) for i, (_, b, c) in enumerate(legs)]
    for cp in inward:
        cp.start()
    for there, on in zip(inward, outward):
        there.wait()
        on.start()
    for cp in outward:
        cp.wait()


def on_device(gradient, left_stat, right_stat, left_root, right_root):
    hbm = pl.BlockSpec(memory_space=pltpu.HBM)
    dma = pltpu.SemaphoreType.DMA
    shapes = (
        jax.ShapeDtypeStruct((ROWS, 2 * PLANE * BLK), BF16),
        jax.ShapeDtypeStruct((QUART, BLK), F32),
        jax.ShapeDtypeStruct((QUART, BLK), F32),
    )
    update, left_new, right_new = pl.pallas_call(
        kernel,
        out_shape=shapes,
        in_specs=[hbm] * 5,
        out_specs=(hbm, hbm, hbm),
        scratch_shapes=[
            pltpu.VMEM((ROWS, 2 * PLANE * BLK), BF16),
            pltpu.VMEM((QUART, BLK), F32),
            pltpu.VMEM((QUART, BLK), F32),
            pltpu.VMEM((ROWS, 2 * PLANE * BLK), BF16),
            pltpu.VMEM((QUART, BLK), F32),
            pltpu.VMEM((QUART, BLK), F32),
            pltpu.VMEM((SUBS, PLANE, 16, PART), BF16),
            pltpu.VMEM((SUBS, PLANE, 16, PART), BF16),
            pltpu.VMEM((SUBS, RING, CHUNK, PART), BF16),
            pltpu.VMEM((SUBS, CHUNK, PART), BF16),
            pltpu.VMEM((2, SUBS, CHUNK, PART), BF16),
            pltpu.VMEM((2, QUART, BLK), BF16),
            pltpu.VMEM((2, QUART, BLK), BF16),
            pltpu.VMEM((BLK, BLK), BF16),
            pltpu.VMEM((BLK, 384), BF16),
            pltpu.VMEM((384, BLK), BF16),
            pltpu.VMEM((384, BLK), BF16),
            pltpu.VMEM((RING, CHUNK, 384), BF16),
            pltpu.VMEM((RING, 8, 128), F32),
            pltpu.VMEM((BLK, BLK), BF16),
            pltpu.VMEM((RING, 48, 384), BF16),
            pltpu.VMEM((RING, 48, 384), BF16),
            pltpu.VMEM((8, 128), F32),
            pltpu.VMEM((RING, 8, 128), F32),
            pltpu.VMEM((2, 8, 128), F32),
            pltpu.VMEM((PLANE, 2, 8, 128), F32),
            pltpu.VMEM((8, 128), F32),
            pltpu.VMEM((SLABS, 8, 128), F32),
            pltpu.VMEM((PLANE, 2, 1, 128), F32),
            pltpu.VMEM((PLANE, 16, WIDE), BF16),
            pltpu.VMEM((PLANE, 16, WIDE), BF16),
            dma((5,)),
            dma((3,)),
            dma((SUBS, PLANE)), dma((SUBS, PLANE)),
            dma((2, 6)), dma((2, 6)),
            dma((5, SUBS)), dma((6, SUBS)),
            dma((5, SUBS)), dma((6, SUBS)),
            dma((2, SUBS)), dma((2, SUBS)),
            dma((RING,)), dma((RING,)),
            dma((RING,)), dma((RING,)),
            dma((PLANE,)), dma((PLANE,)),
            dma((SLABS,)), dma((SLABS,)),
            dma((PLANE,)), dma((PLANE,)),
        ],
        compiler_params=pltpu.CompilerParams(
            collective_id=0, has_side_effects=True, vmem_limit_bytes=63 * 1024 * 1024
        ),
    )(gradient[0], left_stat[0], right_stat[0], left_root[0], right_root[0])
    update, left_new, right_new = pl.pallas_call(
        place_out,
        out_shape=shapes,
        in_specs=[hbm] * 3,
        out_specs=(hbm, hbm, hbm),
        scratch_shapes=[
            pltpu.VMEM((ROWS, 2 * PLANE * BLK), BF16),
            pltpu.VMEM((QUART, BLK), F32),
            pltpu.VMEM((QUART, BLK), F32),
            dma((2, 3)),
        ],
        compiler_params=pltpu.CompilerParams(vmem_limit_bytes=63 * 1024 * 1024),
    )(update, left_new, right_new)
    return (update[None], left_new[None], right_new[None])


def solution(mesh):
    spec = P("mp", "dp", None)
    return jax.shard_map(
        on_device, mesh=mesh, in_specs=(spec,) * 5, out_specs=(spec,) * 3, check_vma=False
    )
```
